32 devices in a mesh: row: 8 (over y, x, core), col: 4 (over z).
Axes of the slice: x: 2, y: 2, z: 4, core: 2. Of those that a mesh axis runs over, the one named last changes fastest.
Arguments:
- samples: bfloat16 [8192, 768], P(('row', 'col')), may hold values from -8 to 8, as said below
Outputs:
- factored: float32 [8192, 8192], P('row', 'col')
The draws below stay inside these ranges and needn't reach their ends.
Inputs may be any that keep to these rules, and one draw needn't show every extreme that they name: `samples`: every entry is a feature value.
All inputs are finite; a program needn't handle non-finite values.
Results may differ from the reference program's by a relative error of at most 0.0003.
Values may be sent and summed in bfloat16 or wider, within the bound.
A program may use at most 128 MiB of HBM per device.

```python
import math
import jax
import jax.numpy as jnp
from jax import lax

FEAT = 768
PANEL = 512
LAYERS = 8
ROWS_DEV = 1024
SAMPLES = 8192
ROW_BLOCK = 64
COL_BLOCK = 128
N_ROW = 8
N_COL = 4


def draw_samples(key, part):
    subkeys = jax.random.split(jax.random.fold_in(key, 11), 7)
    cluster_count = 64
    prototypes = jax.random.normal(subkeys[0], (4, FEAT), jnp.float32)
    mixing = 0.5 * jax.random.normal(subkeys[1], (cluster_count, 4), jnp.float32)
    own_part = jax.random.normal(subkeys[2], (cluster_count, FEAT), jnp.float32)
    centers = jnp.dot(mixing, prototypes) + 0.7 * own_part
    centers = centers / jnp.sqrt(jnp.mean(centers * centers, axis=1, keepdims=True))
    spreads = jnp.exp(jax.random.uniform(subkeys[3], (cluster_count,), jnp.float32, math.log(0.12), math.log(1.0)))
    member = jax.random.randint(subkeys[4], (SAMPLES,), 0, cluster_count)
    flip_sign = jnp.where(jax.random.bernoulli(subkeys[5], 0.5, (SAMPLES,)), 1.0, -1.0)
    noise_part = jax.random.normal(subkeys[6], (SAMPLES, FEAT), jnp.float32)
    row_scales = jnp.ones((SAMPLES,), jnp.float32)
    sample_rows = centers[member] + spreads[member][:, None] * noise_part
    sample_rows = (flip_sign * row_scales)[:, None] * sample_rows
    return jnp.clip(sample_rows, -8.0, 8.0).astype(jnp.bfloat16)


def setup_inputs(seed: int = 0) -> dict:
    streams_of = jax.random.split(jax.random.key(seed), 2)
    return {
        "samples": draw_samples(jax.random.fold_in(streams_of[1], 71), 0),
    }


def ntk_block(left_rows, right_rows, row_ids, col_ids):
    left_f = left_rows.astype(jnp.float32)
    right_f = right_rows.astype(jnp.float32)
    gram_tile = jnp.dot(left_f, right_f.T, precision=lax.Precision.HIGHEST) / FEAT
    row_norms = lax.optimization_barrier(jnp.sum(left_f * left_f, axis=1)) / FEAT
    col_norms = lax.optimization_barrier(jnp.sum(right_f * right_f, axis=1)) / FEAT
    on_diag = row_ids[:, None] == col_ids[None, :]
    norm_scale = jnp.sqrt(row_norms[:, None] * col_norms[None, :])
    covariance = gram_tile
    tangent = gram_tile
    for layer_step in range(LAYERS):
        cosine = jnp.where(on_diag, jnp.float32(1.0), covariance / norm_scale)
        angles = jnp.arccos(cosine)
        sine_part = jnp.sqrt(jnp.maximum(1.0 - cosine * cosine, 0.0))
        covariance = norm_scale / math.pi * (sine_part + (math.pi - angles) * cosine)
        tangent = covariance + tangent * (1.0 - angles / math.pi)
    return tangent / (LAYERS + 1.0) + jnp.where(on_diag, jnp.float32(1.0), jnp.float32(0.0))

def reference(samples):
    blocks = SAMPLES // PANEL
    ordered = samples.reshape(N_ROW, blocks, ROW_BLOCK, FEAT).transpose(1, 0, 2, 3).reshape(SAMPLES, FEAT)
    natural_ids = jnp.arange(SAMPLES, dtype=jnp.int32)
    leading = ntk_block(ordered, ordered[:PANEL], natural_ids, natural_ids[:PANEL])
    corner_factor = jnp.linalg.cholesky(leading[:PANEL])
    solved = lax.linalg.triangular_solve(corner_factor, leading, left_side=False, lower=True, transpose_a=True)
    panel = jnp.concatenate([corner_factor, solved[PANEL:]], axis=0)
    col_ids = natural_ids.reshape(blocks, N_COL, COL_BLOCK).transpose(1, 0, 2).reshape(SAMPLES)
    col_feats = ordered.reshape(blocks, N_COL, COL_BLOCK, FEAT).transpose(1, 0, 2, 3).reshape(SAMPLES, FEAT)
    col_panel = panel.reshape(blocks, N_COL, COL_BLOCK, PANEL).transpose(1, 0, 2, 3).reshape(SAMPLES, PANEL)
    row_ids_all = natural_ids.reshape(blocks, N_ROW, ROW_BLOCK).transpose(1, 0, 2).reshape(SAMPLES)
    row_panel = panel.reshape(blocks, N_ROW, ROW_BLOCK, PANEL).transpose(1, 0, 2, 3).reshape(SAMPLES, PANEL)
    left_index = jnp.minimum(col_ids, PANEL - 1)

    def one_block(block_index):
        start = (block_index * ROWS_DEV).astype(jnp.int32)
        block_rows = lax.dynamic_slice_in_dim(samples, start, ROWS_DEV, 0)
        row_ids = lax.dynamic_slice_in_dim(row_ids_all, start, ROWS_DEV, 0)
        panel_part = lax.dynamic_slice_in_dim(row_panel, start, ROWS_DEV, 0)
        kernel = ntk_block(block_rows, col_feats, row_ids, col_ids)
        update = kernel - jnp.dot(panel_part, col_panel.T, precision=lax.Precision.HIGHEST)
        left_part = jnp.take(panel_part, left_index, axis=1)
        result = jnp.where(col_ids[None, :] < PANEL, left_part, update)
        return jnp.where(row_ids[:, None] >= col_ids[None, :], result, jnp.float32(0.0))
    stacked = lax.map(one_block, jnp.arange(N_ROW, dtype=jnp.int32))
    return stacked.reshape(SAMPLES, SAMPLES)
```

```python
import functools
import math

import jax
import jax.numpy as jnp
from jax import lax
from jax.experimental import pallas as pl
from jax.experimental.pallas import tpu as pltpu
from jax.sharding import PartitionSpec as P

PANEL = 512
LAYERS = 8
CHUNK_ROWS = 64
CHUNK_COLS = 128
TILE_ROWS = 256
TILE_COLS = 512
FACTOR = 128
STRIP = 32
INV_PI = 1.0 / math.pi
ACOS = (
    1.5707963050,
    -0.2145988016,
    0.0889789874,
    -0.0501743046,
    0.0308918810,
    -0.0170881256,
    0.0066700901,
    -0.0012624911,
)
ACOS_PI = tuple(c * INV_PI for c in ACOS)
VMEM_LIMIT = 48 * 1024 * 1024
HIGHEST = lax.Precision.HIGHEST
NT = (((1,), (1,)), ((), ()))
TN = (((0,), (0,)), ((), ()))


def angle_parts(size):
    gap = jnp.maximum(1.0 - size, 1e-30)
    root = gap * lax.rsqrt(gap)
    poly = jnp.full_like(size, ACOS_PI[-1])
    for coefficient in ACOS_PI[-2::-1]:
        poly = poly * size + coefficient
    wide = size * (INV_PI * INV_PI) + (INV_PI * INV_PI)
    sine = root * (wide * lax.rsqrt(wide))
    return root * poly, sine


def tangent_of(raw, on_diag):
    cosine = jnp.where(on_diag, 1.0, raw)
    tangent = raw
    turn, sine = angle_parts(jnp.abs(cosine))
    keep = jnp.where(cosine < 0.0, turn, 1.0 - turn)
    cosine = sine + keep * cosine
    tangent = cosine + tangent * keep
    for _ in range(LAYERS - 1):
        turn, sine = angle_parts(cosine)
        keep = 1.0 - turn
        cosine = sine + keep * cosine
        tangent = cosine + tangent * keep
    return tangent


def ntk_chunk(gram, inv_row, inv_col, len_row, len_col, row_ids, col_ids):
    on_diag = row_ids == col_ids
    raw = gram * inv_row * inv_col
    value = tangent_of(raw, on_diag) * (len_row * len_col)
    return value + jnp.where(on_diag, 1.0, 0.0)


def lengths(feats):
    wide = feats.astype(jnp.float32)
    total = jnp.sum(wide * wide, axis=1)
    scale = math.sqrt(feats.shape[1] * (LAYERS + 1.0))
    return lax.rsqrt(total), jnp.sqrt(total) * (1.0 / scale)


def factor_strip(strip, first):
    place = lax.broadcasted_iota(jnp.int32, (STRIP, 1), 0)
    for j in range(STRIP):
        lane = first + j
        inv = lax.rsqrt(strip[j : j + 1, lane : lane + 1])
        unit = strip[j : j + 1, :] * inv
        col = strip[:, lane : lane + 1] * inv
        col = jnp.where(place > j, col, jnp.where(place == j, col - 1.0, 0.0))
        strip = strip - col * unit
    return strip


def panel_kernel(
    feats, inv_row, inv_col, len_row, len_col, row_ids, col_ids, after, out, work, both
):
    rows = feats.shape[0]
    work[...] = lax.dot_general(
        feats[...], feats[:PANEL, :], NT, preferred_element_type=jnp.float32
    )
    across = PANEL // CHUNK_COLS

    def chunk(k, carry):
        r = k // across
        c = k % across
        needed = jnp.logical_or(
            r * CHUNK_ROWS >= PANEL, (r * CHUNK_ROWS) // FACTOR <= (c * CHUNK_COLS) // FACTOR
        )

        @pl.when(needed)
        def _():
            rs = pl.ds(pl.multiple_of(r * CHUNK_ROWS, CHUNK_ROWS), CHUNK_ROWS)
            cs = pl.ds(pl.multiple_of(c * CHUNK_COLS, CHUNK_COLS), CHUNK_COLS)
            work[rs, cs] = ntk_chunk(
                work[rs, cs], inv_row[rs, :], inv_col[:, cs], len_row[rs, :], len_col[:, cs],
                row_ids[rs, :], col_ids[:, cs],
            )

        return carry

    lax.fori_loop(0, rows // CHUNK_ROWS * across, chunk, 0)
    eye = jnp.where(
        lax.broadcasted_iota(jnp.int32, (FACTOR, FACTOR), 0)
        == lax.broadcasted_iota(jnp.int32, (FACTOR, FACTOR), 1),
        1.0,
        0.0,
    )
    for start in range(0, PANEL, FACTOR):
        stop = start + FACTOR
        both[:, :FACTOR] = work[start:stop, start:stop]
        both[:, FACTOR:] = eye
        for first in range(0, FACTOR, STRIP):
            strip = factor_strip(both[first : first + STRIP, :], first)
            both[first : first + STRIP, :] = strip
            last = first + STRIP
            if last < FACTOR:
                change = lax.dot_general(
                    strip[:, :FACTOR], strip, TN, precision=HIGHEST,
                    preferred_element_type=jnp.float32,
                )
                both[last:, :] = both[last:, :] - change[last:, :]
        inverse = both[:, FACTOR:]
        solved = lax.dot_general(
            work[PANEL:, start:stop], inverse, NT, precision=HIGHEST,
            preferred_element_type=jnp.float32,
        )
        out[:, start:stop] = solved
        if stop < PANEL:
            upper = jnp.dot(
                inverse, work[start:stop, stop:], precision=HIGHEST,
                preferred_element_type=jnp.float32,
            )
            work[stop:PANEL, stop:] = work[stop:PANEL, stop:] - lax.dot_general(
                upper, upper, TN, precision=HIGHEST, preferred_element_type=jnp.float32
            )
            work[PANEL:, stop:] = work[PANEL:, stop:] - jnp.dot(
                solved, upper, precision=HIGHEST, preferred_element_type=jnp.float32
            )


def in_order(pieces):
    shares, blocks = pieces.shape[:2]
    return jnp.concatenate([pieces[s, b] for b in range(blocks) for s in range(shares)], axis=0)


def ntk_kernel(
    row_block, col_block, row_feats, col_feats, inv_row, inv_col, len_row, len_col,
    row_ids, col_ids, after, out,
):
    tile_rows, tile_cols = out.shape
    top = pl.program_id(0) * tile_rows
    left = pl.program_id(1) * tile_cols
    across = tile_cols // CHUNK_COLS

    @pl.when((top + tile_rows - 1) // row_block >= left // col_block)
    def _():
        out[...] = lax.dot_general(
            row_feats[...], in_order(col_feats), NT, preferred_element_type=jnp.float32
        )

        def chunk(k, carry):
            r = (k // across) * CHUNK_ROWS
            c = (k % across) * CHUNK_COLS
            below = (top + r + CHUNK_ROWS - 1) // row_block >= (left + c) // col_block
            beyond = left + c + CHUNK_COLS > col_block

            @pl.when(jnp.logical_and(below, beyond))
            def _():
                rs = pl.ds(pl.multiple_of(r, CHUNK_ROWS), CHUNK_ROWS)
                cs = pl.ds(pl.multiple_of(c, CHUNK_COLS), CHUNK_COLS)
                out[rs, cs] = ntk_chunk(
                    out[rs, cs], inv_row[rs, :], inv_col[:, cs], len_row[rs, :],
                    len_col[:, cs], row_ids[rs, :], col_ids[:, cs],
                )

            return carry

        lax.fori_loop(0, tile_rows // CHUNK_ROWS * across, chunk, 0)


def split(value):
    high = value.astype(jnp.bfloat16)
    return high, (value - high.astype(jnp.float32)).astype(jnp.bfloat16)


def update_kernel(
    row_block, col_block, kernel, panel_row, panel_col, col_index, row_ids, col_ids, out
):
    tile_rows, tile_cols = out.shape
    top = pl.program_id(0) * tile_rows
    left = pl.program_id(1) * tile_cols
    needed = (top + tile_rows - 1) // row_block >= left // col_block

    @pl.when(needed)
    def _():
        row_high, row_low = split(panel_row[...])
        col_high, col_low = split(in_order(panel_col))
        mul = functools.partial(
            lax.dot_general, dimension_numbers=NT, preferred_element_type=jnp.float32
        )
        product = mul(row_high, col_high) + (mul(row_high, col_low) + mul(row_low, col_high))
        result = kernel[...] - product
        out[...] = jnp.where(row_ids[...] >= col_ids[...], result, 0.0)

    @pl.when(jnp.logical_not(needed))
    def _():
        out[...] = jnp.zeros_like(out)

    for member in range(PANEL // col_block):

        @pl.when(jnp.logical_and(left == 0, col_index[0] == member))
        def _():
            part = panel_row[:, member * col_block : (member + 1) * col_block]
            below = row_ids[...] >= col_ids[:, :col_block]
            out[:, :col_block] = jnp.where(below, part, 0.0)


def per_device(samples):
    row_count = lax.axis_size("row")
    col_count = lax.axis_size("col")
    share_count = row_count // col_count
    row_index = lax.axis_index("row")
    col_index = lax.axis_index("col")
    row_block = PANEL // row_count
    col_block = PANEL // col_count
    share_rows, feat_count = samples.shape
    rows_dev = share_rows * col_count
    cols_dev = rows_dev * share_count
    blocks = rows_dev // row_block
    moves = [
        (
            r * col_count + c,
            ((r % share_count) * col_count + c) * col_count + r // share_count,
        )
        for r in range(row_count)
        for c in range(col_count)
    ]

    def spread(moved):
        whole = lax.all_gather(moved, "row", axis=0, tiled=True)
        return whole.reshape(share_count, blocks, row_block, moved.shape[1])

    lead = samples[:row_block]
    held = jnp.where(col_index == 0, lead, jnp.zeros_like(lead))
    for target in range(1, col_count):
        held = held + lax.ppermute(lead, "col", [(0, target)])
    corner_feats = lax.all_gather(held, "row", axis=0, tiled=True)

    moved_feats = lax.ppermute(samples, ("row", "col"), moves)
    row_feats = lax.all_gather(samples, "col", axis=0, tiled=True)
    col_feats = spread(moved_feats)

    local_rows = jnp.arange(rows_dev, dtype=jnp.int32)
    row_ids = local_rows // row_block * PANEL + row_index * row_block + local_rows % row_block
    local_cols = jnp.arange(cols_dev, dtype=jnp.int32)
    col_ids = local_cols // col_block * PANEL + col_index * col_block + local_cols % col_block
    share_ids = lax.dynamic_slice_in_dim(row_ids, col_index * share_rows, share_rows, 0)
    lead_ids = jnp.arange(PANEL, dtype=jnp.int32)

    stacked = jnp.concatenate([corner_feats, samples], axis=0)
    stacked_ids = jnp.concatenate([lead_ids, share_ids], axis=0)
    inv, length = lengths(stacked)
    vmem = pl.BlockSpec(memory_space=pltpu.VMEM)
    solved = pl.pallas_call(
        panel_kernel,
        out_shape=jax.ShapeDtypeStruct((share_rows, PANEL), jnp.float32),
        in_specs=[vmem] * 7 + [pl.BlockSpec(memory_space=pl.ANY)],
        out_specs=vmem,
        scratch_shapes=[
            pltpu.VMEM((PANEL + share_rows, PANEL), jnp.float32),
            pltpu.VMEM((FACTOR, 2 * FACTOR), jnp.float32),
        ],
        compiler_params=pltpu.CompilerParams(vmem_limit_bytes=VMEM_LIMIT),
        cost_estimate=pl.CostEstimate(
            flops=80_000_000_000, bytes_accessed=4_000_000, transcendentals=0
        ),
    )(
        stacked, inv[:, None], inv[None, :PANEL], length[:, None], length[None, :PANEL],
        stacked_ids[:, None], lead_ids[None, :], moved_feats,
    )

    panel_row = lax.all_gather(solved, "col", axis=0, tiled=True)
    panel_col = spread(lax.ppermute(solved, ("row", "col"), moves))

    row_inv, row_len = lengths(row_feats)
    col_inv, col_len = lengths(col_feats.reshape(cols_dev, feat_count))
    col_inv, col_len = (
        value.reshape(share_count, blocks, row_block).transpose(1, 0, 2).reshape(cols_dev)
        for value in (col_inv, col_len)
    )
    tile_rows = min(TILE_ROWS, rows_dev)
    tile_cols = min(TILE_COLS, cols_dev)
    grid = (rows_dev // tile_rows, cols_dev // tile_cols)
    row_one = pl.BlockSpec((tile_rows, 1), lambda i, j: (i, 0))
    col_one = pl.BlockSpec((1, tile_cols), lambda i, j: (0, j))
    tile = pl.BlockSpec((tile_rows, tile_cols), lambda i, j: (i, j))

    def pieces(width):
        shape = (share_count, tile_cols // col_block, row_block, width)
        return pl.BlockSpec(shape, lambda i, j: (0, j, 0, 0))

    params = pltpu.CompilerParams(vmem_limit_bytes=VMEM_LIMIT)
    out_shape = jax.ShapeDtypeStruct((rows_dev, cols_dev), jnp.float32)
    kernel = pl.pallas_call(
        functools.partial(ntk_kernel, row_block, col_block),
        out_shape=out_shape,
        grid=grid,
        in_specs=[
            pl.BlockSpec((tile_rows, feat_count), lambda i, j: (i, 0)),
            pieces(feat_count),
            row_one, col_one, row_one, col_one, row_one, col_one,
            pl.BlockSpec(memory_space=pl.ANY),
        ],
        out_specs=tile,
        compiler_params=params,
        cost_estimate=pl.CostEstimate(
            flops=100_000_000_000, bytes_accessed=16_000_000, transcendentals=0
        ),
    )(
        row_feats, col_feats, row_inv[:, None], col_inv[None, :], row_len[:, None],
        col_len[None, :], row_ids[:, None], col_ids[None, :], solved,
    )
    return pl.pallas_call(
        functools.partial(update_kernel, row_block, col_block),
        out_shape=out_shape,
        grid=grid,
        in_specs=[
            tile,
            pl.BlockSpec((tile_rows, PANEL), lambda i, j: (i, 0)),
            pieces(PANEL),
            pl.BlockSpec(memory_space=pltpu.SMEM),
            row_one, col_one,
        ],
        out_specs=tile,
        input_output_aliases={0: 0},
        compiler_params=params,
        cost_estimate=pl.CostEstimate(
            flops=5_000_000_000, bytes_accessed=20_000_000, transcendentals=0
        ),
    )(kernel, panel_row, panel_col, col_index.astype(jnp.int32)[None], row_ids[:, None], col_ids[None, :])


def solution(mesh):
    return jax.shard_map(
        per_device,
        mesh=mesh,
        in_specs=(P(("row", "col"), None),),
        out_specs=P("row", "col"),
        check_vma=False,
    )
```

```python
import functools
import math

import jax
import jax.numpy as jnp
import numpy as np
from jax import lax
from jax.experimental import pallas as pl
from jax.experimental.pallas import tpu as pltpu
from jax.sharding import PartitionSpec as P

PANEL = 512
LAYERS = 8
CHUNK_ROWS = 64
CHUNK_COLS = 128
TILE_COLS = 512
FACTOR = 128
STRIP = 32
INV_PI = 1.0 / math.pi


def half_turns(reach):
    grid = np.linspace(1e-6, reach, 4001)
    want = 2.0 * np.arcsin(np.sqrt(grid / 2.0)) / (np.sqrt(grid) * math.pi)
    for degree in range(3, 10):
        fit = np.polynomial.Chebyshev.interpolate(
            lambda gap: 2.0 * np.arcsin(np.sqrt(gap / 2.0)) / (np.sqrt(gap) * math.pi),
            degree,
            domain=[0.0, reach],
        ).convert(kind=np.polynomial.Polynomial)
        if np.max(np.abs(fit(grid) - want)) < 4e-8:
            break
    return tuple(float(c) for c in fit.coef)


def layer_polynomials():
    least, found = 0.0, [half_turns(1.0)]
    for _ in range(LAYERS - 1):
        found.append(half_turns(min(1.0, 1.001 - least)))
        angle = math.acos(least)
        least = (math.sin(angle) + (math.pi - angle) * least) / math.pi
    return found


POLYNOMIALS = layer_polynomials()
VMEM_LIMIT = 24 * 1024 * 1024
HIGHEST = lax.Precision.HIGHEST
NT = (((1,), (1,)), ((), ()))
TN = (((0,), (0,)), ((), ()))


def angle_parts(size, polynomial):
    gap = jnp.maximum(1.0 - size, 1e-30)
    root = gap * lax.rsqrt(gap)
    poly = jnp.full_like(size, polynomial[-1])
    for coefficient in polynomial[-2::-1]:
        poly = poly * gap + coefficient
    wide = size * (INV_PI * INV_PI) + (INV_PI * INV_PI)
    sine = root * (wide * lax.rsqrt(wide))
    return root * poly, sine


def tangent_of(raw, on_diag):
    cosine = jnp.where(on_diag, 1.0, raw)
    tangent = raw
    turn, sine = angle_parts(jnp.abs(cosine), POLYNOMIALS[0])
    keep = jnp.where(cosine < 0.0, turn, 1.0 - turn)
    cosine = sine + keep * cosine
    tangent = cosine + tangent * keep
    for polynomial in POLYNOMIALS[1:]:
        turn, sine = angle_parts(cosine, polynomial)
        keep = 1.0 - turn
        cosine = sine + keep * cosine
        tangent = cosine + tangent * keep
    return tangent


def ntk_chunk(gram, inv_row, inv_col, len_row, len_col, row_ids, col_ids):
    on_diag = row_ids == col_ids
    raw = gram * inv_row * inv_col
    value = tangent_of(raw, on_diag) * (len_row * len_col)
    return value + jnp.where(on_diag, 1.0, 0.0)


def lengths(feats):
    wide = feats.astype(jnp.float32)
    total = jnp.sum(wide * wide, axis=1, keepdims=True)
    scale = math.sqrt(feats.shape[1] * (LAYERS + 1.0))
    return lax.rsqrt(total), jnp.sqrt(total) * (1.0 / scale)


def factor_strip(left, right, first):
    place = lax.broadcasted_iota(jnp.int32, (8, FACTOR), 0)
    groups = len(left)
    for g in range(groups):
        cols = [
            [
                jnp.broadcast_to(left[h][:, lane : lane + 1], (8, FACTOR))
                for h in range(g, groups)
            ]
            for lane in range(first + 8 * g, first + 8 * g + 8)
        ]
        for m in range(8):
            inv = lax.rsqrt(cols[m][0][m : m + 1, :])
            scaled = [col * inv for col in cols[m]]
            for n in range(m + 1, 8):
                factor = scaled[0][n : n + 1, :]
                cols[n] = [col - part * factor for col, part in zip(cols[n], scaled)]
            unit_left = left[g][m : m + 1, :] * inv
            unit_right = right[g][m : m + 1, :] * inv
            own = scaled[0]
            scaled[0] = jnp.where(place > m, own, jnp.where(place == m, own - 1.0, 0.0))
            for h in range(g, groups):
                left[h] = left[h] - scaled[h - g] * unit_left
                right[h] = right[h] - scaled[h - g] * unit_right
    return left, right


def panel_kernel(
    feats, inv_row, inv_col, len_row, len_col, row_ids, col_ids, after, work, inverses, both
):
    share_chunks = (feats.shape[0] - PANEL) // CHUNK_ROWS
    work[...] = lax.dot_general(
        feats[...], feats[:PANEL, :], NT, preferred_element_type=jnp.float32
    )
    across = PANEL // CHUNK_COLS

    def fill(rs, cs):
        work[rs, cs] = ntk_chunk(
            work[rs, cs], inv_row[rs, :], inv_col[:, cs], len_row[rs, :], len_col[:, cs],
            row_ids[rs, :], col_ids[:, cs],
        )

    def chunk(k, carry):
        r = k // across
        c = k % across

        @pl.when((r * CHUNK_ROWS) // FACTOR <= (c * CHUNK_COLS) // FACTOR)
        def _():
            fill(
                pl.ds(pl.multiple_of(r * CHUNK_ROWS, CHUNK_ROWS), CHUNK_ROWS),
                pl.ds(pl.multiple_of(c * CHUNK_COLS, CHUNK_COLS), CHUNK_COLS),
            )

        return carry

    lax.fori_loop(0, PANEL // CHUNK_ROWS * across, chunk, 0)
    eye = jnp.where(
        lax.broadcasted_iota(jnp.int32, (FACTOR, FACTOR), 0)
        == lax.broadcasted_iota(jnp.int32, (FACTOR, FACTOR), 1),
        1.0,
        0.0,
    )
    for start in range(0, PANEL, FACTOR):
        stop = start + FACTOR
        both[:, :FACTOR] = work[start:stop, start:stop]
        both[:, FACTOR:] = eye
        for first in range(0, FACTOR, STRIP):
            for q in range(first // STRIP, share_chunks, FACTOR // STRIP):
                own = PANEL + q * CHUNK_ROWS
                fill(pl.ds(own, CHUNK_ROWS), pl.ds(start, FACTOR))
            strip = both[first : first + STRIP, :]
            left, right = factor_strip(
                [strip[r : r + 8, :FACTOR] for r in range(0, STRIP, 8)],
                [strip[r : r + 8, FACTOR:] for r in range(0, STRIP, 8)],
                first,
            )
            left = jnp.concatenate(left, axis=0)
            strip = jnp.concatenate([left, jnp.concatenate(right, axis=0)], axis=1)
            both[first : first + STRIP, :] = strip
            last = first + STRIP
            if last < FACTOR:
                change = lax.dot_general(
                    left, strip, TN, precision=HIGHEST,
                    preferred_element_type=jnp.float32,
                )
                both[last:, :] = both[last:, :] - change[last:, :]
        inverse = both[:, FACTOR:]
        inverses[start:stop, :] = inverse
        if stop < PANEL:
            upper = jnp.dot(
                inverse, work[start:stop, stop:], precision=HIGHEST,
                preferred_element_type=jnp.float32,
            )
            work[stop:PANEL, stop:] = work[stop:PANEL, stop:] - lax.dot_general(
                upper, upper, TN, precision=HIGHEST, preferred_element_type=jnp.float32
            )
            work[start:stop, stop:] = upper


def solve_kernel(work, inverses, *rest):
    out = rest[-1]
    for start in range(0, PANEL, FACTOR):
        stop = start + FACTOR
        part = work[PANEL:, start:stop]
        if start:
            part = part - jnp.dot(
                out[:, :start], work[:start, start:stop], precision=HIGHEST,
                preferred_element_type=jnp.float32,
            )
        out[:, start:stop] = lax.dot_general(
            part, inverses[start:stop, :], NT, precision=HIGHEST,
            preferred_element_type=jnp.float32,
        )


def in_order(pieces):
    shares, blocks = pieces.shape[:2]
    return jnp.concatenate([pieces[s, b] for b in range(blocks) for s in range(shares)], axis=0)


def first_needed(j, tile_rows, tile_cols, row_block, col_block):
    return j * tile_cols // col_block * row_block // tile_rows


def ntk_kernel(
    row_block, col_block, col_feats, inv_col, len_col, row_ids, col_ids, col_index, after, *rest
):
    *pieces, out, row_feats, inv_row, len_row = rest
    tile_rows, tile_cols = out.shape
    i = pl.program_id(1)
    top = i * tile_rows
    left = pl.program_id(0) * tile_cols
    across = tile_cols // CHUNK_COLS
    count = len(pieces)

    for step, piece in enumerate(pieces):

        @pl.when(jnp.logical_and(left == 0, (col_index[0] - i + count) % count == step))
        def _():
            row_feats[i] = piece[...]
            inv, length = lengths(piece[...])
            inv_row[i] = inv
            len_row[i] = length

    @pl.when((top + tile_rows - 1) // row_block >= left // col_block)
    def _():
        out[...] = lax.dot_general(
            row_feats[i], in_order(col_feats), NT, preferred_element_type=jnp.float32
        )

        def chunk(k, carry):
            r = (k // across) * CHUNK_ROWS
            c = (k % across) * CHUNK_COLS
            below = (top + r + CHUNK_ROWS - 1) // row_block >= (left + c) // col_block
            beyond = left + c + CHUNK_COLS > col_block

            @pl.when(jnp.logical_and(below, beyond))
            def _():
                rs = pl.ds(pl.multiple_of(r, CHUNK_ROWS), CHUNK_ROWS)
                cs = pl.ds(pl.multiple_of(c, CHUNK_COLS), CHUNK_COLS)
                out[rs, cs] = ntk_chunk(
                    out[rs, cs], inv_row[i, rs, :], inv_col[:, cs], len_row[i, rs, :],
                    len_col[:, cs], row_ids[rs, :], col_ids[:, cs],
                )

            return carry

        lax.fori_loop(0, tile_rows // CHUNK_ROWS * across, chunk, 0)


def split(value):
    high = value.astype(jnp.bfloat16)
    return high, (value - high.astype(jnp.float32)).astype(jnp.bfloat16)


def update_kernel(
    row_block, col_block, kernel, panel_col, col_index, row_ids, col_ids, *rest
):
    *pieces, out, row_high, row_low = rest
    tile_rows, tile_cols = out.shape
    i = pl.program_id(1)
    top = i * tile_rows
    left = pl.program_id(0) * tile_cols
    needed = (top + tile_rows - 1) // row_block >= left // col_block
    count = len(pieces)

    for step, piece in enumerate(pieces):

        @pl.when(jnp.logical_and(left == 0, (col_index[0] - i + count) % count == step))
        def _():
            row_high[i], row_low[i] = split(piece[...])

    @pl.when(needed)
    def _():
        col_high, col_low = split(in_order(panel_col))
        mul = functools.partial(
            lax.dot_general, dimension_numbers=NT, preferred_element_type=jnp.float32
        )
        high, low = row_high[i], row_low[i]
        product = mul(high, col_high) + (mul(high, col_low) + mul(low, col_high))
        result = kernel[...] - product
        out[...] = jnp.where(row_ids[...] >= col_ids[...], result, 0.0)

    @pl.when(jnp.logical_not(needed))
    def _():
        out[...] = jnp.zeros_like(out)

    for member in range(count):
        for step, piece in enumerate(pieces):

            @pl.when(
                (left == 0) & (col_index[0] == member) & ((member - i + count) % count == step)
            )
            def _():
                part = piece[:, member * col_block : (member + 1) * col_block]
                below = row_ids[...] >= col_ids[:, :col_block]
                out[:, :col_block] = jnp.where(below, part, 0.0)


def per_device(samples):
    row_count = lax.axis_size("row")
    col_count = lax.axis_size("col")
    share_count = row_count // col_count
    row_index = lax.axis_index("row")
    col_index = lax.axis_index("col")
    row_block = PANEL // row_count
    col_block = PANEL // col_count
    share_rows, feat_count = samples.shape
    rows_dev = share_rows * col_count
    cols_dev = rows_dev * share_count
    blocks = rows_dev // row_block
    moves = [
        (
            r * col_count + c,
            ((r % share_count) * col_count + c) * col_count + r // share_count,
        )
        for r in range(row_count)
        for c in range(col_count)
    ]

    def spread(moved):
        whole = lax.all_gather(moved, "row", axis=0, tiled=True)
        return whole.reshape(share_count, blocks, row_block, moved.shape[1])

    lead = samples[:row_block]
    held = jnp.where(col_index == 0, lead, jnp.zeros_like(lead))
    for target in range(1, col_count):
        held = held + lax.ppermute(lead, "col", [(0, target)])
    corner_feats = lax.all_gather(held, "row", axis=0, tiled=True)

    def pass_along(share):
        return [share] + [
            lax.ppermute(share, "col", [(k, (k + s) % col_count) for k in range(col_count)])
            for s in range(1, col_count)
        ]

    late_samples, _ = lax.optimization_barrier((samples, held))
    moved_feats = lax.ppermute(late_samples, ("row", "col"), moves)
    row_feats = pass_along(late_samples)
    col_feats = spread(moved_feats)

    local_rows = jnp.arange(rows_dev, dtype=jnp.int32)
    row_ids = local_rows // row_block * PANEL + row_index * row_block + local_rows % row_block
    local_cols = jnp.arange(cols_dev, dtype=jnp.int32)
    col_ids = local_cols // col_block * PANEL + col_index * col_block + local_cols % col_block
    share_ids = lax.dynamic_slice_in_dim(row_ids, col_index * share_rows, share_rows, 0)
    lead_ids = jnp.arange(PANEL, dtype=jnp.int32)

    stacked = jnp.concatenate([corner_feats, samples], axis=0)
    stacked_ids = jnp.concatenate([lead_ids, share_ids], axis=0)
    inv, length = lengths(stacked)
    vmem = pl.BlockSpec(memory_space=pltpu.VMEM)
    work, inverses = pl.pallas_call(
        panel_kernel,
        out_shape=[
            jax.ShapeDtypeStruct((PANEL + share_rows, PANEL), jnp.float32),
            jax.ShapeDtypeStruct((PANEL, FACTOR), jnp.float32),
        ],
        in_specs=[vmem] * 7 + [pl.BlockSpec(memory_space=pl.ANY)],
        out_specs=[vmem, vmem],
        scratch_shapes=[
            pltpu.VMEM((FACTOR, 2 * FACTOR), jnp.float32),
        ],
        compiler_params=pltpu.CompilerParams(vmem_limit_bytes=VMEM_LIMIT),
        cost_estimate=pl.CostEstimate(
            flops=80_000_000_000, bytes_accessed=4_000_000, transcendentals=0
        ),
    )(
        stacked, inv, inv[:PANEL].reshape(1, PANEL), length, length[:PANEL].reshape(1, PANEL),
        stacked_ids[:, None], lead_ids[None, :], moved_feats,
    )
    solved = pl.pallas_call(
        solve_kernel,
        out_shape=jax.ShapeDtypeStruct((share_rows, PANEL), jnp.float32),
        in_specs=[vmem] * 2 + [pl.BlockSpec(memory_space=pl.ANY)] * (col_count - 1),
        out_specs=vmem,
        compiler_params=pltpu.CompilerParams(vmem_limit_bytes=VMEM_LIMIT),
        cost_estimate=pl.CostEstimate(
            flops=5_000_000_000, bytes_accessed=4_000_000, transcendentals=0
        ),
    )(work, inverses, *row_feats[1:])

    panel_row = pass_along(solved)
    panel_col = spread(lax.ppermute(solved, ("row", "col"), moves))

    col_inv, col_len = lengths(col_feats.reshape(cols_dev, feat_count))
    col_inv, col_len = (
        value.reshape(share_count, blocks, row_block).transpose(1, 0, 2).reshape(1, cols_dev)
        for value in (col_inv, col_len)
    )
    tile_rows = share_rows
    tile_cols = min(TILE_COLS, cols_dev)
    grid = (cols_dev // tile_cols, rows_dev // tile_rows)
    first = functools.partial(
        first_needed, tile_rows=tile_rows, tile_cols=tile_cols, row_block=row_block,
        col_block=col_block,
    )
    row_one = pl.BlockSpec((tile_rows, 1), lambda j, i: (i, 0))
    col_one = pl.BlockSpec((1, tile_cols), lambda j, i: (0, j))
    tile = pl.BlockSpec((tile_rows, tile_cols), lambda j, i: (i, j))
    needed_tile = pl.BlockSpec(
        (tile_rows, tile_cols), lambda j, i: (jnp.maximum(i, first(j)), j)
    )
    scalar = pl.BlockSpec(memory_space=pltpu.SMEM)
    col_place = col_index.astype(jnp.int32)[None]

    def share(width):
        return pl.BlockSpec((share_rows, width), lambda j, i: (0, 0))

    def pieces(width):
        shape = (share_count, tile_cols // col_block, row_block, width)
        return pl.BlockSpec(shape, lambda j, i: (0, j, 0, 0))

    params = pltpu.CompilerParams(vmem_limit_bytes=VMEM_LIMIT)
    out_shape = jax.ShapeDtypeStruct((rows_dev, cols_dev), jnp.float32)
    kernel = pl.pallas_call(
        functools.partial(ntk_kernel, row_block, col_block),
        out_shape=out_shape,
        grid=grid,
        in_specs=[
            pieces(feat_count),
            col_one, col_one, row_one, col_one, scalar,
            pl.BlockSpec(memory_space=pl.ANY),
        ]
        + [share(feat_count)] * col_count,
        out_specs=needed_tile,
        scratch_shapes=[
            pltpu.VMEM((col_count, share_rows, feat_count), jnp.bfloat16),
            pltpu.VMEM((col_count, share_rows, 1), jnp.float32),
            pltpu.VMEM((col_count, share_rows, 1), jnp.float32),
        ],
        compiler_params=params,
        cost_estimate=pl.CostEstimate(
            flops=100_000_000_000, bytes_accessed=16_000_000, transcendentals=0
        ),
    )(
        col_feats, col_inv, col_len, row_ids[:, None], col_ids[None, :], col_place, solved,
        *row_feats,
    )

    return pl.pallas_call(
        functools.partial(update_kernel, row_block, col_block),
        out_shape=out_shape,
        grid=grid,
        in_specs=[
            needed_tile,
            pieces(PANEL),
            scalar,
            row_one, col_one,
        ]
        + [share(PANEL)] * col_count,
        out_specs=tile,
        scratch_shapes=[
            pltpu.VMEM((col_count, share_rows, PANEL), jnp.bfloat16),
            pltpu.VMEM((col_count, share_rows, PANEL), jnp.bfloat16),
        ],
        compiler_params=params,
        cost_estimate=pl.CostEstimate(
            flops=5_000_000_000, bytes_accessed=20_000_000, transcendentals=0
        ),
    )(kernel, panel_col, col_place, row_ids[:, None], col_ids[None, :], *panel_row)


def solution(mesh):
    return jax.shard_map(
        per_device,
        mesh=mesh,
        in_specs=(P(("row", "col"), None),),
        out_specs=P("row", "col"),
        check_vma=False,
    )
```

```python
import functools
import math

import jax
import jax.numpy as jnp
import numpy as np
from jax import lax
from jax.experimental import pallas as pl
from jax.experimental.pallas import tpu as pltpu
from jax.sharding import PartitionSpec as P

PANEL = 512
LAYERS = 8
CHUNK_ROWS = 64
CHUNK_COLS = 128
TILE_COLS = 512
FACTOR = 128
STRIP = 32
INV_PI = 1.0 / math.pi


def half_turns(reach):
    grid = np.linspace(1e-6, reach, 4001)
    want = 2.0 * np.arcsin(np.sqrt(grid / 2.0)) / (np.sqrt(grid) * math.pi)
    for degree in range(3, 10):
        fit = np.polynomial.Chebyshev.interpolate(
            lambda gap: 2.0 * np.arcsin(np.sqrt(gap / 2.0)) / (np.sqrt(gap) * math.pi),
            degree,
            domain=[0.0, reach],
        ).convert(kind=np.polynomial.Polynomial)
        if np.max(np.abs(fit(grid) - want)) < 4e-8:
            break
    return tuple(float(c) for c in fit.coef)


def layer_polynomials():
    least, found = 0.0, [half_turns(1.0)]
    for _ in range(LAYERS - 1):
        found.append(half_turns(min(1.0, 1.001 - least)))
        angle = math.acos(least)
        least = (math.sin(angle) + (math.pi - angle) * least) / math.pi
    return found


POLYNOMIALS = layer_polynomials()
VMEM_LIMIT = 24 * 1024 * 1024
HIGHEST = lax.Precision.HIGHEST
NT = (((1,), (1,)), ((), ()))
TN = (((0,), (0,)), ((), ()))


def angle_parts(size, polynomial):
    gap = jnp.maximum(1.0 - size, 1e-30)
    root = gap * lax.rsqrt(gap)
    poly = jnp.full_like(size, polynomial[-1])
    for coefficient in polynomial[-2::-1]:
        poly = poly * gap + coefficient
    wide = size * (INV_PI * INV_PI) + (INV_PI * INV_PI)
    sine = root * (wide * lax.rsqrt(wide))
    return root * poly, sine


def tangent_of(raw, on_diag):
    cosine = jnp.where(on_diag, 1.0, raw)
    tangent = raw
    turn, sine = angle_parts(jnp.abs(cosine), POLYNOMIALS[0])
    keep = jnp.where(cosine < 0.0, turn, 1.0 - turn)
    cosine = sine + keep * cosine
    tangent = cosine + tangent * keep
    for polynomial in POLYNOMIALS[1:]:
        turn, sine = angle_parts(cosine, polynomial)
        keep = 1.0 - turn
        cosine = sine + keep * cosine
        tangent = cosine + tangent * keep
    return tangent


def ntk_chunk(gram, inv_row, inv_col, len_row, len_col, row_ids, col_ids):
    on_diag = row_ids == col_ids
    raw = gram * inv_row * inv_col
    value = tangent_of(raw, on_diag) * (len_row * len_col)
    return value + jnp.where(on_diag, 1.0, 0.0)


def lengths(feats):
    wide = feats.astype(jnp.float32)
    total = jnp.sum(wide * wide, axis=1, keepdims=True)
    scale = math.sqrt(feats.shape[1] * (LAYERS + 1.0))
    return lax.rsqrt(total), jnp.sqrt(total) * (1.0 / scale)


def factor_strip(left, right, first):
    place = lax.broadcasted_iota(jnp.int32, (8, FACTOR), 0)
    groups = len(left)
    for g in range(groups):
        cols = [
            [
                jnp.broadcast_to(left[h][:, lane : lane + 1], (8, FACTOR))
                for h in range(g, groups)
            ]
            for lane in range(first + 8 * g, first + 8 * g + 8)
        ]
        for m in range(8):
            inv = lax.rsqrt(cols[m][0][m : m + 1, :])
            scaled = [col * inv for col in cols[m]]
            for n in range(m + 1, 8):
                factor = scaled[0][n : n + 1, :]
                cols[n] = [col - part * factor for col, part in zip(cols[n], scaled)]
            unit_left = left[g][m : m + 1, :] * inv
            unit_right = right[g][m : m + 1, :] * inv
            own = scaled[0]
            scaled[0] = jnp.where(place > m, own, jnp.where(place == m, own - 1.0, 0.0))
            for h in range(g, groups):
                left[h] = left[h] - scaled[h - g] * unit_left
                right[h] = right[h] - scaled[h - g] * unit_right
    return left, right


def panel_kernel(
    feats, inv_row, inv_col, len_row, len_col, row_ids, col_ids, after, work, inverses, both
):
    share_chunks = (feats.shape[0] - PANEL) // CHUNK_ROWS
    work[...] = lax.dot_general(
        feats[...], feats[:PANEL, :], NT, preferred_element_type=jnp.float32
    )
    across = PANEL // CHUNK_COLS

    def fill(rs, cs):
        work[rs, cs] = ntk_chunk(
            work[rs, cs], inv_row[rs, :], inv_col[:, cs], len_row[rs, :], len_col[:, cs],
            row_ids[rs, :], col_ids[:, cs],
        )

    def chunk(k, carry):
        r = k // across
        c = k % across

        @pl.when((r * CHUNK_ROWS) // FACTOR <= (c * CHUNK_COLS) // FACTOR)
        def _():
            fill(
                pl.ds(pl.multiple_of(r * CHUNK_ROWS, CHUNK_ROWS), CHUNK_ROWS),
                pl.ds(pl.multiple_of(c * CHUNK_COLS, CHUNK_COLS), CHUNK_COLS),
            )

        return carry

    lax.fori_loop(0, PANEL // CHUNK_ROWS * across, chunk, 0)
    eye = jnp.where(
        lax.broadcasted_iota(jnp.int32, (FACTOR, FACTOR), 0)
        == lax.broadcasted_iota(jnp.int32, (FACTOR, FACTOR), 1),
        1.0,
        0.0,
    )
    for start in range(0, PANEL, FACTOR):
        stop = start + FACTOR
        both[:, :FACTOR] = work[start:stop, start:stop]
        both[:, FACTOR:] = eye
        for first in range(0, FACTOR, STRIP):
            for q in range(first // STRIP, share_chunks, FACTOR // STRIP):
                own = PANEL + q * CHUNK_ROWS
                fill(pl.ds(own, CHUNK_ROWS), pl.ds(start, FACTOR))
            strip = both[first : first + STRIP, :]
            left, right = factor_strip(
                [strip[r : r + 8, :FACTOR] for r in range(0, STRIP, 8)],
                [strip[r : r + 8, FACTOR:] for r in range(0, STRIP, 8)],
                first,
            )
            left = jnp.concatenate(left, axis=0)
            strip = jnp.concatenate([left, jnp.concatenate(right, axis=0)], axis=1)
            both[first : first + STRIP, :] = strip
            last = first + STRIP
            if last < FACTOR:
                change = lax.dot_general(
                    left, strip, TN, precision=HIGHEST,
                    preferred_element_type=jnp.float32,
                )
                both[last:, :] = both[last:, :] - change[last:, :]
        inverse = both[:, FACTOR:]
        inverses[start:stop, :] = inverse
        if stop < PANEL:
            upper = jnp.dot(
                inverse, work[start:stop, stop:], precision=HIGHEST,
                preferred_element_type=jnp.float32,
            )
            work[stop:PANEL, stop:] = work[stop:PANEL, stop:] - lax.dot_general(
                upper, upper, TN, precision=HIGHEST, preferred_element_type=jnp.float32
            )
            work[start:stop, stop:] = upper


def solve_kernel(work, inverses, *rest):
    out = rest[-1]
    for start in range(0, PANEL, FACTOR):
        stop = start + FACTOR
        part = work[PANEL:, start:stop]
        if start:
            part = part - jnp.dot(
                out[:, :start], work[:start, start:stop], precision=HIGHEST,
                preferred_element_type=jnp.float32,
            )
        out[:, start:stop] = lax.dot_general(
            part, inverses[start:stop, :], NT, precision=HIGHEST,
            preferred_element_type=jnp.float32,
        )


def in_order(pieces):
    shares, blocks = pieces.shape[:2]
    return jnp.concatenate([pieces[s, b] for b in range(blocks) for s in range(shares)], axis=0)


def first_needed(j, tile_rows, tile_cols, row_block, col_block):
    return j * tile_cols // col_block * row_block // tile_rows


def ntk_kernel(
    row_block, col_block, col_feats, row_ids, col_ids, col_index, after, *rest
):
    *pieces, out, row_feats, inv_row, len_row, inv_col, len_col = rest
    tile_rows, tile_cols = out.shape
    i = pl.program_id(1)
    top = i * tile_rows
    left = pl.program_id(0) * tile_cols
    across = tile_cols // CHUNK_COLS
    count = len(pieces)

    for step, piece in enumerate(pieces):

        @pl.when(jnp.logical_and(left == 0, (col_index[0] - i + count) % count == step))
        def _():
            row_feats[i] = piece[...]
            inv, length = lengths(piece[...])
            inv_row[i] = inv
            len_row[i] = length

    @pl.when(i == 0)
    def _():
        wide = in_order(col_feats).astype(jnp.float32)
        high, low = split(wide * wide)
        ones = jnp.ones((8, wide.shape[1]), jnp.bfloat16)
        total = lax.dot_general(ones, high, NT, preferred_element_type=jnp.float32)
        total += lax.dot_general(ones, low, NT, preferred_element_type=jnp.float32)
        inv_col[...] = lax.rsqrt(total)
        len_col[...] = jnp.sqrt(total) * (1.0 / math.sqrt(wide.shape[1] * (LAYERS + 1.0)))

    @pl.when((top + tile_rows - 1) // row_block >= left // col_block)
    def _():
        out[...] = lax.dot_general(
            row_feats[i], in_order(col_feats), NT, preferred_element_type=jnp.float32
        )

        def chunk(k, carry):
            r = (k // across) * CHUNK_ROWS
            c = (k % across) * CHUNK_COLS
            below = (top + r + CHUNK_ROWS - 1) // row_block >= (left + c) // col_block
            beyond = left + c + CHUNK_COLS > col_block

            @pl.when(jnp.logical_and(below, beyond))
            def _():
                rs = pl.ds(pl.multiple_of(r, CHUNK_ROWS), CHUNK_ROWS)
                cs = pl.ds(pl.multiple_of(c, CHUNK_COLS), CHUNK_COLS)
                out[rs, cs] = ntk_chunk(
                    out[rs, cs], inv_row[i, rs, :], inv_col[:1, cs], len_row[i, rs, :],
                    len_col[:1, cs], row_ids[rs, :], col_ids[:, cs],
                )

            return carry

        lax.fori_loop(0, tile_rows // CHUNK_ROWS * across, chunk, 0)


def split(value):
    high = value.astype(jnp.bfloat16)
    return high, (value - high.astype(jnp.float32)).astype(jnp.bfloat16)


def update_kernel(
    row_block, col_block, kernel, panel_col, col_index, row_ids, col_ids, *rest
):
    *pieces, out, row_high, row_low = rest
    tile_rows, tile_cols = out.shape
    i = pl.program_id(1)
    top = i * tile_rows
    left = pl.program_id(0) * tile_cols
    needed = (top + tile_rows - 1) // row_block >= left // col_block
    count = len(pieces)

    for step, piece in enumerate(pieces):

        @pl.when(jnp.logical_and(left == 0, (col_index[0] - i + count) % count == step))
        def _():
            row_high[i], row_low[i] = split(piece[...])

    @pl.when(needed)
    def _():
        col_high, col_low = split(in_order(panel_col))
        mul = functools.partial(
            lax.dot_general, dimension_numbers=NT, preferred_element_type=jnp.float32
        )
        high, low = row_high[i], row_low[i]
        product = mul(high, col_high) + (mul(high, col_low) + mul(low, col_high))
        result = kernel[...] - product
        out[...] = jnp.where(row_ids[...] >= col_ids[...], result, 0.0)

    @pl.when(jnp.logical_not(needed))
    def _():
        out[...] = jnp.zeros_like(out)

    for member in range(count):
        for step, piece in enumerate(pieces):

            @pl.when(
                (left == 0) & (col_index[0] == member) & ((member - i + count) % count == step)
            )
            def _():
                part = piece[:, member * col_block : (member + 1) * col_block]
                below = row_ids[...] >= col_ids[:, :col_block]
                out[:, :col_block] = jnp.where(below, part, 0.0)


def per_device(samples):
    row_count = lax.axis_size("row")
    col_count = lax.axis_size("col")
    share_count = row_count // col_count
    row_index = lax.axis_index("row")
    col_index = lax.axis_index("col")
    row_block = PANEL // row_count
    col_block = PANEL // col_count
    share_rows, feat_count = samples.shape
    rows_dev = share_rows * col_count
    cols_dev = rows_dev * share_count
    blocks = rows_dev // row_block
    moves = [
        (
            r * col_count + c,
            ((r % share_count) * col_count + c) * col_count + r // share_count,
        )
        for r in range(row_count)
        for c in range(col_count)
    ]

    def spread(moved):
        whole = lax.all_gather(moved, "row", axis=0, tiled=True)
        return whole.reshape(share_count, blocks, row_block, moved.shape[1])

    lead = samples[:row_block]
    held = jnp.where(col_index == 0, lead, jnp.zeros_like(lead))
    for target in range(1, col_count):
        held = held + lax.ppermute(lead, "col", [(0, target)])
    corner_feats = lax.all_gather(held, "row", axis=0, tiled=True)

    def pass_along(share):
        return [share] + [
            lax.ppermute(share, "col", [(k, (k + s) % col_count) for k in range(col_count)])
            for s in range(1, col_count)
        ]

    late_samples, _ = lax.optimization_barrier((samples, held))
    moved_feats = lax.ppermute(late_samples, ("row", "col"), moves)
    later_samples, moved_feats = lax.optimization_barrier((late_samples, moved_feats))
    row_feats = pass_along(later_samples)
    col_feats = spread(moved_feats)

    local_rows = jnp.arange(rows_dev, dtype=jnp.int32)
    row_ids = local_rows // row_block * PANEL + row_index * row_block + local_rows % row_block
    local_cols = jnp.arange(cols_dev, dtype=jnp.int32)
    col_ids = local_cols // col_block * PANEL + col_index * col_block + local_cols % col_block
    share_ids = lax.dynamic_slice_in_dim(row_ids, col_index * share_rows, share_rows, 0)
    lead_ids = jnp.arange(PANEL, dtype=jnp.int32)

    stacked = jnp.concatenate([corner_feats, samples], axis=0)
    stacked_ids = jnp.concatenate([lead_ids, share_ids], axis=0)
    inv, length = lengths(stacked)
    vmem = pl.BlockSpec(memory_space=pltpu.VMEM)
    work, inverses = pl.pallas_call(
        panel_kernel,
        out_shape=[
            jax.ShapeDtypeStruct((PANEL + share_rows, PANEL), jnp.float32),
            jax.ShapeDtypeStruct((PANEL, FACTOR), jnp.float32),
        ],
        in_specs=[vmem] * 7 + [pl.BlockSpec(memory_space=pl.ANY)],
        out_specs=[vmem, vmem],
        scratch_shapes=[
            pltpu.VMEM((FACTOR, 2 * FACTOR), jnp.float32),
        ],
        compiler_params=pltpu.CompilerParams(vmem_limit_bytes=VMEM_LIMIT),
        cost_estimate=pl.CostEstimate(
            flops=80_000_000_000, bytes_accessed=4_000_000, transcendentals=0
        ),
    )(
        stacked, inv, inv[:PANEL].reshape(1, PANEL), length, length[:PANEL].reshape(1, PANEL),
        stacked_ids[:, None], lead_ids[None, :], moved_feats,
    )
    solved = pl.pallas_call(
        solve_kernel,
        out_shape=jax.ShapeDtypeStruct((share_rows, PANEL), jnp.float32),
        in_specs=[vmem] * 2 + [pl.BlockSpec(memory_space=pl.ANY)] * (col_count - 1),
        out_specs=vmem,
        compiler_params=pltpu.CompilerParams(vmem_limit_bytes=VMEM_LIMIT),
        cost_estimate=pl.CostEstimate(
            flops=5_000_000_000, bytes_accessed=4_000_000, transcendentals=0
        ),
    )(work, inverses, *row_feats[1:])

    moved_panel = lax.ppermute(solved, ("row", "col"), moves)
    later_solved, moved_panel = lax.optimization_barrier((solved, moved_panel))
    panel_row = pass_along(later_solved)
    panel_col = spread(moved_panel)

    tile_rows = share_rows
    tile_cols = min(TILE_COLS, cols_dev)
    grid = (cols_dev // tile_cols, rows_dev // tile_rows)
    first = functools.partial(
        first_needed, tile_rows=tile_rows, tile_cols=tile_cols, row_block=row_block,
        col_block=col_block,
    )
    row_one = pl.BlockSpec((tile_rows, 1), lambda j, i: (i, 0))
    col_one = pl.BlockSpec((1, tile_cols), lambda j, i: (0, j))
    tile = pl.BlockSpec((tile_rows, tile_cols), lambda j, i: (i, j))
    needed_tile = pl.BlockSpec(
        (tile_rows, tile_cols), lambda j, i: (jnp.maximum(i, first(j)), j)
    )
    scalar = pl.BlockSpec(memory_space=pltpu.SMEM)
    col_place = col_index.astype(jnp.int32)[None]

    def share(width):
        return pl.BlockSpec((share_rows, width), lambda j, i: (0, 0))

    def pieces(width):
        shape = (share_count, tile_cols // col_block, row_block, width)
        return pl.BlockSpec(shape, lambda j, i: (0, j, 0, 0))

    params = pltpu.CompilerParams(vmem_limit_bytes=2 * VMEM_LIMIT)
    out_shape = jax.ShapeDtypeStruct((rows_dev, cols_dev), jnp.float32)
    kernel = pl.pallas_call(
        functools.partial(ntk_kernel, row_block, col_block),
        out_shape=out_shape,
        grid=grid,
        in_specs=[
            pieces(feat_count),
            row_one, col_one, scalar,
            pl.BlockSpec(memory_space=pl.ANY),
        ]
        + [share(feat_count)] * col_count,
        out_specs=needed_tile,
        scratch_shapes=[
            pltpu.VMEM((col_count, share_rows, feat_count), jnp.bfloat16),
            pltpu.VMEM((col_count, share_rows, 1), jnp.float32),
            pltpu.VMEM((col_count, share_rows, 1), jnp.float32),
            pltpu.VMEM((8, tile_cols), jnp.float32),
            pltpu.VMEM((8, tile_cols), jnp.float32),
        ],
        compiler_params=params,
        cost_estimate=pl.CostEstimate(
            flops=100_000_000_000, bytes_accessed=16_000_000, transcendentals=0
        ),
    )(
        col_feats, row_ids[:, None], col_ids[None, :], col_place, solved,
        *row_feats,
    )

    return pl.pallas_call(
        functools.partial(update_kernel, row_block, col_block),
        out_shape=out_shape,
        grid=grid,
        in_specs=[
            needed_tile,
            pieces(PANEL),
            scalar,
            row_one, col_one,
        ]
        + [share(PANEL)] * col_count,
        out_specs=tile,
        scratch_shapes=[
            pltpu.VMEM((col_count, share_rows, PANEL), jnp.bfloat16),
            pltpu.VMEM((col_count, share_rows, PANEL), jnp.bfloat16),
        ],
        compiler_params=params,
        cost_estimate=pl.CostEstimate(
            flops=5_000_000_000, bytes_accessed=20_000_000, transcendentals=0
        ),
    )(kernel, panel_col, col_place, row_ids[:, None], col_ids[None, :], *panel_row)


def solution(mesh):
    return jax.shard_map(
        per_device,
        mesh=mesh,
        in_specs=(P(("row", "col"), None),),
        out_specs=P("row", "col"),
        check_vma=False,
    )
```
